32 devices in a mesh: req: 4 (over y, x), tm: 8 (over z, core).
Axes of the slice: x: 2, y: 2, z: 4, core: 2. Of those that a mesh axis runs over, the one named last changes fastest.
Arguments:
- latents: bfloat16 [32, 12288], P('req', 'tm'), may hold values from -6 to 6
- lengths: int32 [2], replicated, may hold values from 1 to 21, 32 in all
- w_in: bfloat16 [3, 3, 3, 16, 384], replicated, may hold values from -0.3125 to 0.3125
- b_in: float32 [384], replicated, may hold values from -3 to 3
- w_mid: bfloat16 [3, 3, 3, 384, 384], replicated, may hold values from -0.0625 to 0.0625
- b_mid: float32 [384], replicated, may hold values from -3 to 3
Outputs:
- decoded: bfloat16 [32, 64, 48, 384], P(('req', 'tm'))
The draws below stay inside these ranges and needn't reach their ends.
Inputs may be any that keep to these rules, and one draw needn't show every extreme that they name: Request lengths in latent frames, in order along the frames, summing to 32; the longest has exactly 21.
All inputs are finite; a program needn't handle non-finite values.
Results may differ from the reference program's by a relative error of at most 0.0041.
Values may be sent and summed in bfloat16 or wider, within the bound.
A program may use at most 192 MiB of HBM per device.

```python
import math
import jax
import jax.numpy as jnp
import numpy as np
from jax import lax

C = 16
CH = 384
HT = 32
WT = 24
MOST = 21
FRAMES = 32
REQS = 2


def shard_levels(stream_key, dims, cuts, smallest, largest):
    def one(axis_at, shards_of):
        steps = jax.random.uniform(jax.random.fold_in(jax.random.fold_in(stream_key, 6), axis_at), (shards_of,), jnp.float32, smallest / len(cuts), largest / len(cuts))
        return jnp.repeat(jnp.exp(steps), dims[axis_at] // shards_of).reshape((-1,) + (1,) * (len(dims) - axis_at - 1))

    factor_of = one(*cuts[0])
    for cut in cuts[1:]:
        factor_of = factor_of * one(*cut)
    return factor_of


def profile(amount, total, bound, lean):
    weights = [(1 << 20) // math.isqrt(standing ** lean) + 1 for standing in range(2, amount + 1)]
    spare, given = total - bound - (amount - 1), [1] * (amount - 1)
    while spare > 0:
        free = [i for i in range(amount - 1) if given[i] < bound]
        pool, budget = sum([weights[i] for i in free]), spare
        for i in free:
            more = min(bound - given[i], max(1, budget * weights[i] // pool), spare)
            given[i] = given[i] + more
            spare = spare - more
    return np.array([bound] + given)


def ragged(stream_key, number_of, total, reach, skew):
    if number_of == 2:
        one = jax.random.randint(stream_key, (), max(1, total - reach), min(reach, total - 1) + 1)
        return jnp.stack([one, total - one])
    sizes = jnp.asarray(profile(number_of, total, reach, skew), jnp.int32)
    pairs = (number_of - 1) // 2
    giver, taker = sizes[1:1 + 2 * pairs:2], sizes[2:2 + 2 * pairs:2]
    slack = jnp.minimum(giver - 1, reach - taker)
    moved = jax.random.randint(jax.random.fold_in(stream_key, 1), (pairs,), 0, 1 << 20) % (slack + 1)
    sizes = sizes.at[1:1 + 2 * pairs:2].set(giver - moved).at[2:2 + 2 * pairs:2].set(taker + moved)
    return sizes[jax.random.permutation(jax.random.fold_in(stream_key, 2), number_of)]


def scatter_about(stream_key, shape, deviation, bound, split=(), kind=jnp.bfloat16):
    entries = jax.random.normal(stream_key, shape, jnp.float32) * deviation
    if len(split) > 0:
        entries = shard_levels(stream_key, shape, split, -0.22, 0.18) * entries
    return jnp.clip(entries, min=-bound, max=bound).astype(kind)


def setup_inputs(seed: int = 0) -> dict:
    keys = jax.random.split(jax.random.key(seed), 7)
    latents = scatter_about(keys[0], (FRAMES, HT * WT * C), 1.0, 6.0, ((0, 4), (1, 8)))
    lengths = ragged(keys[1], REQS, FRAMES, MOST, 2).astype(jnp.int32)
    w_in = scatter_about(keys[2], (3, 3, 3, C, CH), (27 * C) ** -0.5, 0.3125)
    b_in = scatter_about(keys[3], (CH,), 0.5, 3.0, (), jnp.float32)
    w_mid = scatter_about(keys[4], (3, 3, 3, CH, CH), (27 * CH) ** -0.5, 0.0625)
    b_mid = scatter_about(keys[5], (CH,), 0.5, 3.0, (), jnp.float32)
    return {"latents": latents, "lengths": lengths, "w_in": w_in, "b_in": b_in, "w_mid": w_mid, "b_mid": b_mid}


def request_of(position, request_ends):
    return jnp.sum((position[:, None] >= request_ends[None, :]).astype(jnp.int32), axis=1)


def keep_taps(position, request_ends):
    own_request = request_of(position, request_ends)
    columns = []
    for offset in (2, 1):
        earlier = position - offset
        matches = (earlier >= 0) & (request_of(earlier, request_ends) == own_request)
        columns.append(matches.astype(jnp.bfloat16))
    columns.append(jnp.ones_like(columns[0]))
    return jnp.stack(columns, axis=1)


def causal_conv(window, tap_mask, weight, bias):
    out_frames = window.shape[0] - 2
    height = window.shape[1] - 2
    breadth = window.shape[2] - 2
    in_chan = window.shape[3]
    out_chan = weight.shape[-1]
    summed = jnp.zeros((out_frames * height * breadth, out_chan), jnp.float32)
    for time_tap in range(3):
        tap_keep = tap_mask[:, time_tap][:, None, None, None]
        for row_tap in range(3):
            columns = jnp.concatenate(
                [window[time_tap:time_tap + out_frames, row_tap:row_tap + height, col_tap:col_tap + breadth, :]
                 for col_tap in range(3)], axis=-1) * tap_keep
            summed = summed + jnp.dot(columns.reshape(out_frames * height * breadth, 3 * in_chan),
                                      weight[time_tap, row_tap].reshape(3 * in_chan, out_chan),
                                      preferred_element_type=jnp.float32)
    return (summed + bias[None, :]).reshape(out_frames, height, breadth, out_chan)


def upsample(field):
    return jnp.repeat(jnp.repeat(field, 2, axis=1), 2, axis=2)


def run_conv(frames_all, tap_mask, weight, bias):
    padded = jnp.pad(frames_all, ((2, 0), (1, 1), (1, 1), (0, 0)))

    def one_frame(index):
        window = lax.dynamic_slice_in_dim(padded, index, 3, 0)
        taps = lax.dynamic_slice_in_dim(tap_mask, index, 1, 0)
        return causal_conv(window, taps, weight, bias)[0]

    return lax.map(one_frame, jnp.arange(frames_all.shape[0], dtype=jnp.int32))


def reference(latents, lengths, w_in, b_in, w_mid, b_mid):
    latent = latents.reshape(FRAMES, HT, WT, C)
    request_ends = jnp.cumsum(lengths).astype(jnp.int32)
    tap_mask = keep_taps(jnp.arange(FRAMES, dtype=jnp.int32), request_ends)
    hidden = jax.nn.silu(run_conv(latent, tap_mask, w_in, b_in)).astype(jnp.bfloat16)
    decoded = run_conv(upsample(hidden), tap_mask, w_mid, b_mid)
    return decoded.astype(jnp.bfloat16)
```

```python
import functools

import jax
import jax.numpy as jnp
from jax import lax
from jax.experimental import pallas as pl
from jax.experimental.pallas import tpu as pltpu
from jax.sharding import PartitionSpec as P

F32 = jnp.float32
BF16 = jnp.bfloat16
MESH = pl.DeviceIdType.MESH
REACH = 4


def exchange_kernel(groups, members, lat_ref, out_ref, recv, send_sem, recv_sem, own_sem):
    r = lax.axis_index("req")
    me = lax.axis_index("tm")
    slots = REACH + 1
    has_next = r + 1 < groups
    has_prev = r > 0
    nxt = jnp.minimum(r + 1, groups - 1)
    prv = jnp.maximum(r - 1, 0)

    barrier = pltpu.get_barrier_semaphore()
    for t in range(members):

        @pl.when(me != t)
        def _():
            pl.semaphore_signal(barrier, inc=1, device_id=(r, jnp.int32(t)), device_id_type=MESH)

    @pl.when(has_prev & (me < REACH))
    def _():
        for t in range(members):
            pl.semaphore_signal(barrier, inc=1, device_id=(prv, jnp.int32(t)), device_id_type=MESH)

    @pl.when(has_next)
    def _():
        pl.semaphore_wait(barrier, members - 1 + REACH)

    @pl.when(jnp.logical_not(has_next))
    def _():
        pl.semaphore_wait(barrier, members - 1)

    def within(t, sender):
        count = min(t, REACH) + 1
        return lat_ref.at[pl.ds(t + 1 - count, count)], recv.at[sender, pl.ds(slots - count, count)]

    def across(t, sender):
        count = REACH - t
        return lat_ref.at[pl.ds(members - count, count)], recv.at[sender, pl.ds(0, count)]

    def near_copy(t):
        src, dst = within(t, me)
        return pltpu.make_async_remote_copy(
            src_ref=src,
            dst_ref=dst,
            send_sem=send_sem.at[t],
            recv_sem=recv_sem.at[0, me],
            device_id=(r, jnp.int32(t)),
            device_id_type=MESH,
        )

    def far_copy(t):
        src, dst = across(t, me)
        return pltpu.make_async_remote_copy(
            src_ref=src,
            dst_ref=dst,
            send_sem=send_sem.at[members + t],
            recv_sem=recv_sem.at[1, me],
            device_id=(nxt, jnp.int32(t)),
            device_id_type=MESH,
        )

    @pl.when(has_next)
    def _():
        for t in range(REACH):
            far_copy(t).start()

    for t in range(members):

        @pl.when(me != t)
        def _():
            near_copy(t).start()

        @pl.when(me == t)
        def _():
            src, dst = within(t, t)
            own = pltpu.make_async_copy(src, dst, own_sem)
            own.start()
            own.wait()

    for t in range(members):

        @pl.when(me == t)
        def _():
            for sender in range(members):
                if sender != t:
                    src, dst = within(t, sender)
                    pltpu.make_async_copy(src, dst, recv_sem.at[0, sender]).wait()
            if t < REACH:

                @pl.when(has_prev)
                def _():
                    for sender in range(members):
                        src, dst = across(t, sender)
                        pltpu.make_async_copy(src, dst, recv_sem.at[1, sender]).wait()

                @pl.when(jnp.logical_not(has_prev))
                def _():
                    for sender in range(members):
                        recv[sender, 0 : REACH - t] = jnp.zeros(
                            (REACH - t,) + recv.shape[2:], recv.dtype
                        )

    rows = recv.shape[2]
    for sender in range(members):
        for s in range(slots):
            out_ref[s, sender * rows : (sender + 1) * rows, :] = recv[sender, s].astype(F32)

    for t in range(members):

        @pl.when(me != t)
        def _():
            near_copy(t).wait_send()

    @pl.when(has_next)
    def _():
        for t in range(REACH):
            far_copy(t).wait_send()


def exchange(latents, groups, members, line):
    frames, feats = latents.shape
    rows = feats // line
    slots = REACH + 1
    pieces = latents.reshape(frames, rows, line)
    return pl.pallas_call(
        functools.partial(exchange_kernel, groups, members),
        out_shape=jax.ShapeDtypeStruct((slots, rows * members, line), F32),
        in_specs=[pl.BlockSpec(memory_space=pltpu.VMEM)],
        out_specs=pl.BlockSpec(memory_space=pltpu.VMEM),
        scratch_shapes=[
            pltpu.VMEM((members, slots, rows, line), BF16),
            pltpu.SemaphoreType.DMA((members + REACH,)),
            pltpu.SemaphoreType.DMA((2, members)),
            pltpu.SemaphoreType.DMA,
        ],
        compiler_params=pltpu.CompilerParams(collective_id=0, has_side_effects=True),
        name="exchange",
    )(pieces)


def decode_kernel(
    members, steps, ht, wt, c, ch,
    lengths_ref, x_ref, w_in_ref, b_in_ref, w_mid_ref, b_mid_ref, out_ref,
    raw, ws, wd, lh, ld, hb, sl, wide, raw_sem,
):
    step = pl.program_id(0)
    pos = ht * wt
    k_all = 3 * ch
    per = 128 // ht
    frame = lax.axis_index("req") * members + lax.axis_index("tm")

    def request_of(f):
        end = jnp.int32(0)
        count = jnp.int32(0)
        for r in range(lengths_ref.shape[0]):
            end = end + lengths_ref[r]
            count = count + (f >= end).astype(jnp.int32)
        return count

    def linked(earlier, f):
        return ((earlier >= 0) & (request_of(earlier) == request_of(f))) | (earlier == f)

    @pl.when(step == 0)
    def _prologue():
        for a in range(3):
            pltpu.make_async_copy(w_mid_ref.at[a], raw.at[a], raw_sem.at[a]).start()

        row_id = lax.broadcasted_iota(jnp.int32, (ht, wt * c), 0)
        quarter = lax.broadcasted_iota(jnp.int32, (c, 128), 1) // ht

        def spread(s, carry):
            x = jnp.where(frame - REACH + s >= 0, x_ref[s], 0.0)
            above = jnp.where(row_id == 0, 0.0, pltpu.roll(x, 1, 0))
            below = jnp.where(row_id == ht - 1, 0.0, pltpu.roll(x, ht - 1, 0))
            stacked = jnp.concatenate([above, x, below] + [jnp.zeros_like(x)] * (per - 3), axis=0)
            turned = stacked.T
            rolled = [turned] + [pltpu.roll(turned, ht * n, 1) for n in range(1, per)]
            zero = jnp.zeros((c, 128), F32)
            for di in range(3):
                for dj in range(3):
                    for jb in range(wt // per):
                        piece = zero
                        for jj in range(per):
                            j = jb * per + jj + dj - 1
                            if 0 <= j < wt:
                                part = rolled[(jj - di) % per][j * c : (j + 1) * c, :]
                                piece = jnp.where(quarter == jj, part, piece)
                        sl[s, pl.ds((di * 3 + dj) * c, c), pl.ds(jb * 128, 128)] = piece.astype(BF16)
            return carry

        lax.fori_loop(0, REACH + 1, spread, 0)

        edge = jnp.zeros((ht, 128), F32)
        for n in range(ch // 128):
            hb[n, pl.ds(0, ht, stride=wt), :] = edge
            hb[n, pl.ds(2 * pos + wt - 1, ht, stride=wt), :] = edge

        def first_layer(g, carry):
            f = frame - 2 + g
            acc = jnp.zeros((pos, ch), F32)
            for a in range(3):
                keep = linked(f - 2 + a, f)
                w = w_in_ref[a]
                w = jnp.where(keep, w, jnp.zeros_like(w))
                acc = acc + lax.dot_general(
                    sl[g + a], w, (((0,), (0,)), ((), ())), preferred_element_type=F32
                )
            v = acc + b_in_ref[...]
            h = (v / (1.0 + jnp.exp(-v))).astype(BF16).astype(F32)
            h = jnp.where(linked(f, frame), h, 0.0)
            for j in range(wt):
                for n in range(ch // 128):
                    part = h[j * ht : (j + 1) * ht, n * 128 : (n + 1) * 128]
                    hb[n, pl.ds(pos + j, ht, stride=wt), :] = part
                    if j < wt - 1:
                        hb[n, pl.ds(j + 1, ht, stride=wt), :] = part
                    if j > 0:
                        hb[n, pl.ds(2 * pos + j - 1, ht, stride=wt), :] = part
            z = jnp.zeros((wt, 128), F32)
            rest = jnp.zeros((ld.shape[0] - pos - wt, 128), F32)
            for v_at in range(3):
                for n in range(ch // 128):
                    lane = pl.ds(pl.multiple_of(v_at * k_all + g * ch + n * 128, 128), 128)
                    x = hb[n, pl.ds(v_at * pos, pos), :]
                    lh[:, lane] = x.astype(BF16)
                    d = jnp.concatenate([x, z, rest], 0) - jnp.concatenate([z, x, rest], 0)
                    ld[:, lane] = d.astype(BF16)
            return carry

        lax.fori_loop(0, 3, first_layer, 0)

        chunk = 32
        for a in range(3):
            pltpu.make_async_copy(w_mid_ref.at[a], raw.at[a], raw_sem.at[a]).wait()

            def combine(n, carry):
                at = pl.multiple_of(n * chunk, chunk)
                w = [[raw[a, p, q, pl.ds(at, chunk), :].astype(F32) for q in range(3)] for p in range(3)]
                s = [w[0][q] + w[1][q] + w[2][q] for q in range(3)]

                def columns(t):
                    return ((t[0], t[1] + t[2]), (t[0] + t[1], t[2]))

                s_c, u_c, l_c = columns(s), columns(w[0]), columns(w[2])
                for b in range(2):
                    for v in range(2):
                        dst = pl.ds(pl.multiple_of(v * k_all + a * ch + at, chunk), chunk)
                        ws[b, dst, :] = s_c[b][v].astype(BF16)
                        wd[b, dst, pl.ds(0, ch)] = u_c[b][v].astype(BF16)
                        wd[b, dst, pl.ds(ch, ch)] = l_c[b][v].astype(BF16)
                return carry

            lax.fori_loop(0, ch // chunk, combine, 0)

    lines = ht // steps
    m = lines * wt
    m_ext = m + 2 * 16
    row0 = pl.multiple_of(step * m, 16)
    for b in range(2):
        lane = pl.ds(b * k_all, 2 * k_all)
        ys = jnp.dot(lh[pl.ds(row0, m), lane], ws[b], preferred_element_type=F32) + b_mid_ref[...]
        yd = jnp.dot(ld[pl.ds(row0, m_ext), lane], wd[b], preferred_element_type=F32)
        y = (ys - yd[0:m, 0:ch], ys + yd[wt : wt + m, ch : 2 * ch])
        for i in range(lines):
            for a in range(2):
                for n in range(ch // 128):
                    wide[n, pl.ds((2 * i + a) * 2 * wt + b, wt, stride=2), :] = y[a][
                        i * wt : (i + 1) * wt, n * 128 : (n + 1) * 128
                    ]
    for i in range(2 * lines):
        for n in range(ch // 128):
            out_ref[i, :, n * 128 : (n + 1) * 128] = wide[n, pl.ds(i * 2 * wt, 2 * wt), :].astype(BF16)


def decode(x, lengths, w_in, b_in, w_mid, b_mid, members):
    slots, ht, line = x.shape
    c, ch = w_in.shape[-2:]
    wt = line // c
    pos = ht * wt
    steps = 2
    m = pos // steps
    vmem = pl.BlockSpec(memory_space=pltpu.VMEM)
    return pl.pallas_call(
        functools.partial(decode_kernel, members, steps, ht, wt, c, ch),
        grid=(steps,),
        out_shape=jax.ShapeDtypeStruct((2 * ht, 2 * wt, ch), BF16),
        in_specs=[
            pl.BlockSpec(memory_space=pltpu.SMEM),
            vmem, vmem, vmem,
            pl.BlockSpec(memory_space=pl.ANY),
            vmem,
        ],
        out_specs=pl.BlockSpec((2 * ht // steps, 2 * wt, ch), lambda i: (i, 0, 0)),
        scratch_shapes=[
            pltpu.VMEM(w_mid.shape, BF16),
            pltpu.VMEM((2, 6 * ch, ch), BF16),
            pltpu.VMEM((2, 6 * ch, 2 * ch), BF16),
            pltpu.VMEM((pos, 9 * ch), BF16),
            pltpu.VMEM((pos + 32, 9 * ch), BF16),
            pltpu.VMEM((ch // 128, 3 * pos, 128), F32),
            pltpu.VMEM((slots, 9 * c, pos), BF16),
            pltpu.VMEM((ch // 128, 4 * m, 128), F32),
            pltpu.SemaphoreType.DMA((3,)),
        ],
        compiler_params=pltpu.CompilerParams(vmem_limit_bytes=60 * 1024 * 1024),
        name="decode",
    )(lengths, x, w_in.reshape(3, 9 * c, ch), b_in.reshape(1, ch), w_mid, b_mid.reshape(1, ch))


def solution(mesh):
    groups, members = mesh.shape["req"], mesh.shape["tm"]

    def on_device(latents, lengths, w_in, b_in, w_mid, b_mid):
        c = w_in.shape[-2]
        line = 24 * c
        x = exchange(latents, groups, members, line)
        return decode(x, lengths, w_in, b_in, w_mid, b_mid, members)[None]

    in_specs = (P("req", "tm"), P(), P(), P(), P(), P())
    out_specs = P(("req", "tm"), None, None, None)
    return jax.shard_map(
        on_device, mesh=mesh, in_specs=in_specs, out_specs=out_specs, check_vma=False
    )
```

```python
import functools

import jax
import jax.numpy as jnp
from jax import lax
from jax.experimental import pallas as pl
from jax.experimental.pallas import tpu as pltpu
from jax.sharding import PartitionSpec as P

F32 = jnp.float32
BF16 = jnp.bfloat16
MESH = pl.DeviceIdType.MESH
REACH = 4


def exchange_kernel(
    groups, members, line,
    lat_ref, w_mid_ref, out_ref, ws, wd,
    stage, recv, raw, send_sem, recv_sem, own_sem, raw_sem,
):
    r = lax.axis_index("req")
    me = lax.axis_index("tm")
    slots = REACH + 1
    has_next = r + 1 < groups
    has_prev = r > 0
    nxt = jnp.minimum(r + 1, groups - 1)
    prv = jnp.maximum(r - 1, 0)

    ch = w_mid_ref.shape[-1]
    k_all = 3 * ch
    for a in range(3):
        pltpu.make_async_copy(w_mid_ref.at[a], raw.at[a], raw_sem.at[a]).start()

    barrier = pltpu.get_barrier_semaphore()
    for t in range(members):

        @pl.when(me != t)
        def _():
            pl.semaphore_signal(barrier, inc=1, device_id=(r, jnp.int32(t)), device_id_type=MESH)

    @pl.when(has_prev & (me < REACH))
    def _():
        for t in range(members):
            pl.semaphore_signal(barrier, inc=1, device_id=(prv, jnp.int32(t)), device_id_type=MESH)

    mine = lat_ref[...].astype(F32)
    for u in range(lat_ref.shape[0]):
        stage[u] = mine[u : u + 1, :].astype(BF16)

    @pl.when(has_next)
    def _():
        pl.semaphore_wait(barrier, members - 1 + REACH)

    @pl.when(jnp.logical_not(has_next))
    def _():
        pl.semaphore_wait(barrier, members - 1)

    def within(t, sender):
        count = min(t, REACH) + 1
        return stage.at[pl.ds(t + 1 - count, count)], recv.at[sender, pl.ds(slots - count, count)]

    def across(t, sender):
        count = REACH - t
        return stage.at[pl.ds(members - count, count)], recv.at[sender, pl.ds(0, count)]

    def near_copy(t):
        src, dst = within(t, me)
        return pltpu.make_async_remote_copy(
            src_ref=src,
            dst_ref=dst,
            send_sem=send_sem.at[t],
            recv_sem=recv_sem.at[0, me],
            device_id=(r, jnp.int32(t)),
            device_id_type=MESH,
        )

    def far_copy(t):
        src, dst = across(t, me)
        return pltpu.make_async_remote_copy(
            src_ref=src,
            dst_ref=dst,
            send_sem=send_sem.at[members + t],
            recv_sem=recv_sem.at[1, me],
            device_id=(nxt, jnp.int32(t)),
            device_id_type=MESH,
        )

    @pl.when(has_next)
    def _():
        for t in range(REACH):
            far_copy(t).start()

    for t in range(members):

        @pl.when(me != t)
        def _():
            near_copy(t).start()

        @pl.when(me == t)
        def _():
            src, dst = within(t, t)
            own = pltpu.make_async_copy(src, dst, own_sem)
            own.start()
            own.wait()

    chunk = 32
    for a in range(3):
        pltpu.make_async_copy(w_mid_ref.at[a], raw.at[a], raw_sem.at[a]).wait()
        def combine(n, carry):
            at = pl.multiple_of(n * chunk, chunk)
            w = [[raw[a, p, q, pl.ds(at, chunk), :].astype(F32) for q in range(3)] for p in range(3)]
            s = [w[0][q] + w[1][q] + w[2][q] for q in range(3)]

            def columns(t):
                return ((t[0], t[1] + t[2]), (t[0] + t[1], t[2]))

            s_c, u_c, l_c = columns(s), columns(w[0]), columns(w[2])
            for b in range(2):
                for v in range(2):
                    dst = pl.ds(pl.multiple_of(v * k_all + a * ch + at, chunk), chunk)
                    ws[b, dst, :] = s_c[b][v].astype(BF16)
                    wd[b, dst, pl.ds(0, ch)] = u_c[b][v].astype(BF16)
                    wd[b, dst, pl.ds(ch, ch)] = l_c[b][v].astype(BF16)
            return carry

        lax.fori_loop(0, ch // chunk, combine, 0)


    for t in range(members):

        @pl.when(me == t)
        def _():
            for sender in range(members):
                if sender != t:
                    src, dst = within(t, sender)
                    pltpu.make_async_copy(src, dst, recv_sem.at[0, sender]).wait()
            if t < REACH:

                @pl.when(has_prev)
                def _():
                    for sender in range(members):
                        src, dst = across(t, sender)
                        pltpu.make_async_copy(src, dst, recv_sem.at[1, sender]).wait()

                @pl.when(jnp.logical_not(has_prev))
                def _():
                    for sender in range(members):
                        recv[sender, 0 : REACH - t] = jnp.zeros(
                            (REACH - t,) + recv.shape[2:], recv.dtype
                        )

    rows = recv.shape[-1] // line
    for sender in range(members):
        for s in range(slots):
            piece = recv[sender, s].astype(F32)
            for n in range(rows):
                out_ref[s, pl.ds(sender * rows + n, 1), :] = piece[:, n * line : (n + 1) * line]

    for t in range(members):

        @pl.when(me != t)
        def _():
            near_copy(t).wait_send()

    @pl.when(has_next)
    def _():
        for t in range(REACH):
            far_copy(t).wait_send()


def exchange(latents, w_mid, groups, members, line):
    frames, feats = latents.shape
    rows = feats // line
    slots = REACH + 1
    ch = w_mid.shape[-1]
    vmem = pl.BlockSpec(memory_space=pltpu.VMEM)
    hbm = pl.BlockSpec(memory_space=pl.ANY)
    ws = (2, 6 * ch, ch)
    wd = (2, 6 * ch, 2 * ch)
    return pl.pallas_call(
        functools.partial(exchange_kernel, groups, members, line),
        out_shape=(
            jax.ShapeDtypeStruct((slots, rows * members, line), F32),
            jax.ShapeDtypeStruct(ws, BF16),
            jax.ShapeDtypeStruct(wd, BF16),
        ),
        in_specs=[vmem, hbm],
        out_specs=(vmem, vmem, vmem),
        scratch_shapes=[
            pltpu.VMEM((frames, 1, feats), BF16),
            pltpu.VMEM((members, slots, 1, feats), BF16),
            pltpu.VMEM(w_mid.shape, BF16),
            pltpu.SemaphoreType.DMA((members + REACH,)),
            pltpu.SemaphoreType.DMA((2, members)),
            pltpu.SemaphoreType.DMA,
            pltpu.SemaphoreType.DMA((3,)),
        ],
        compiler_params=pltpu.CompilerParams(
            collective_id=0, has_side_effects=True, vmem_limit_bytes=46 * 1024 * 1024
        ),
        name="exchange",
    )(latents, w_mid)


def decode_kernel(
    members, steps, ht, wt, c, ch,
    lengths_ref, x_ref, w_in_ref, b_in_ref, ws, wd, b_mid_ref, out_ref,
    lh, ld, hb, sl, wide,
):
    step = pl.program_id(0)
    pos = ht * wt
    k_all = 3 * ch
    per = 128 // ht
    frame = lax.axis_index("req") * members + lax.axis_index("tm")

    def request_of(f):
        end = jnp.int32(0)
        count = jnp.int32(0)
        for r in range(lengths_ref.shape[0]):
            end = end + lengths_ref[r]
            count = count + (f >= end).astype(jnp.int32)
        return count

    def linked(earlier, f):
        return ((earlier >= 0) & (request_of(earlier) == request_of(f))) | (earlier == f)

    @pl.when(step == 0)
    def _prologue():
        row_id = lax.broadcasted_iota(jnp.int32, (ht, wt * c), 0)
        quarter = lax.broadcasted_iota(jnp.int32, (c, 128), 1) // ht

        def spread(s, carry):
            x = jnp.where(frame - REACH + s >= 0, x_ref[s], 0.0)
            above = jnp.where(row_id == 0, 0.0, pltpu.roll(x, 1, 0))
            below = jnp.where(row_id == ht - 1, 0.0, pltpu.roll(x, ht - 1, 0))
            stacked = jnp.concatenate([above, x, below] + [jnp.zeros_like(x)] * (per - 3), axis=0)
            turned = stacked.T
            rolled = [turned] + [pltpu.roll(turned, ht * n, 1) for n in range(1, per)]
            zero = jnp.zeros((c, 128), F32)
            for di in range(3):
                for dj in range(3):
                    for jb in range(wt // per):
                        piece = zero
                        for jj in range(per):
                            j = jb * per + jj + dj - 1
                            if 0 <= j < wt:
                                part = rolled[(jj - di) % per][j * c : (j + 1) * c, :]
                                piece = jnp.where(quarter == jj, part, piece)
                        at = pl.multiple_of(s * 9 * c + (di * 3 + dj) * c, c)
                        sl[pl.ds(at, c), pl.ds(jb * 128, 128)] = piece.astype(BF16)
            return carry

        lax.fori_loop(0, REACH + 1, spread, 0)

        edge = jnp.zeros((ht, 128), F32)
        for n in range(ch // 128):
            hb[n, pl.ds(0, ht, stride=wt), :] = edge
            hb[n, pl.ds(2 * pos + wt - 1, ht, stride=wt), :] = edge

        def first_layer(g, carry):
            f = frame - 2 + g
            taps = []
            for a in range(3):
                w = w_in_ref[a]
                taps.append(jnp.where(linked(f - 2 + a, f), w, jnp.zeros_like(w)))
            acc = lax.dot_general(
                sl[pl.ds(pl.multiple_of(g * 9 * c, c), 27 * c), :],
                jnp.concatenate(taps, 0),
                (((0,), (0,)), ((), ())),
                preferred_element_type=F32,
            )
            v = acc + b_in_ref[...][None, :]
            h = (v * (0.5 + 0.5 * jnp.tanh(0.5 * v))).astype(BF16).astype(F32)
            h = jnp.where(linked(f, frame), h, 0.0)
            for j in range(wt):
                for n in range(ch // 128):
                    part = h[j * ht : (j + 1) * ht, n * 128 : (n + 1) * 128]
                    hb[n, pl.ds(pos + j, ht, stride=wt), :] = part
                    if j < wt - 1:
                        hb[n, pl.ds(j + 1, ht, stride=wt), :] = part
                    if j > 0:
                        hb[n, pl.ds(2 * pos + j - 1, ht, stride=wt), :] = part
            z = jnp.zeros((wt, 128), F32)
            rest = jnp.zeros((ld.shape[0] - pos - wt, 128), F32)
            for v_at in range(3):
                for n in range(ch // 128):
                    lane = pl.ds(pl.multiple_of(v_at * k_all + g * ch + n * 128, 128), 128)
                    x = hb[n, pl.ds(v_at * pos, pos), :]
                    lh[:, lane] = x.astype(BF16)
                    d = jnp.concatenate([x, z, rest], 0) - jnp.concatenate([z, x, rest], 0)
                    ld[:, lane] = d.astype(BF16)
            return carry

        lax.fori_loop(0, 3, first_layer, 0)


    lines = ht // steps
    m = lines * wt
    m_ext = m + 2 * 16
    row0 = pl.multiple_of(step * m, 16)
    for b in range(2):
        lane = pl.ds(b * k_all, 2 * k_all)
        ys = jnp.dot(lh[pl.ds(row0, m), lane], ws[b], preferred_element_type=F32) + b_mid_ref[...][None, :]
        yd = jnp.dot(ld[pl.ds(row0, m_ext), lane], wd[b], preferred_element_type=F32)
        y = (ys - yd[0:m, 0:ch], ys + yd[wt : wt + m, ch : 2 * ch])
        for i in range(lines):
            for a in range(2):
                for n in range(ch // 128):
                    wide[n, pl.ds((2 * i + a) * 2 * wt + b, wt, stride=2), :] = y[a][
                        i * wt : (i + 1) * wt, n * 128 : (n + 1) * 128
                    ]
    for i in range(2 * lines):
        for n in range(ch // 128):
            out_ref[i, :, n * 128 : (n + 1) * 128] = wide[n, pl.ds(i * 2 * wt, 2 * wt), :].astype(BF16)


def decode(x, lengths, w_in, b_in, ws, wd, b_mid, members):
    slots, ht, line = x.shape
    c, ch = w_in.shape[-2:]
    wt = line // c
    pos = ht * wt
    steps = 2
    m = pos // steps
    vmem = pl.BlockSpec(memory_space=pltpu.VMEM)
    return pl.pallas_call(
        functools.partial(decode_kernel, members, steps, ht, wt, c, ch),
        grid=(steps,),
        out_shape=jax.ShapeDtypeStruct((2 * ht, 2 * wt, ch), BF16),
        in_specs=[
            pl.BlockSpec(memory_space=pltpu.SMEM),
            vmem, vmem, vmem, vmem, vmem, vmem,
        ],
        out_specs=pl.BlockSpec((2 * ht // steps, 2 * wt, ch), lambda i: (i, 0, 0)),
        scratch_shapes=[
            pltpu.VMEM((pos, 9 * ch), BF16),
            pltpu.VMEM((pos + 32, 9 * ch), BF16),
            pltpu.VMEM((ch // 128, 3 * pos, 128), F32),
            pltpu.VMEM((slots * 9 * c, pos), BF16),
            pltpu.VMEM((ch // 128, 4 * m, 128), F32),
        ],
        compiler_params=pltpu.CompilerParams(vmem_limit_bytes=40 * 1024 * 1024),
        name="decode",
    )(lengths, x, w_in.reshape(3, 9 * c, ch), b_in, ws, wd, b_mid)


def solution(mesh):
    groups, members = mesh.shape["req"], mesh.shape["tm"]

    def on_device(latents, lengths, w_in, b_in, w_mid, b_mid):
        c = w_in.shape[-2]
        line = 24 * c
        x, ws, wd = exchange(latents, w_mid, groups, members, line)
        return decode(x, lengths, w_in, b_in, ws, wd, b_mid, members)[None]

    in_specs = (P("req", "tm"), P(), P(), P(), P(), P())
    out_specs = P(("req", "tm"), None, None, None)
    return jax.shard_map(
        on_device, mesh=mesh, in_specs=in_specs, out_specs=out_specs, check_vma=False
    )
```

```python
import functools

import jax
import jax.numpy as jnp
from jax import lax
from jax.experimental import pallas as pl
from jax.experimental.pallas import tpu as pltpu
from jax.sharding import PartitionSpec as P

F32 = jnp.float32
BF16 = jnp.bfloat16
MESH = pl.DeviceIdType.MESH
REACH = 4


def exchange_kernel(
    groups, members, line,
    lat_ref, w_mid_ref, out_ref, ws, wd,
    stage, recv, raw, send_sem, recv_sem, own_sem, raw_sem,
):
    r = lax.axis_index("req")
    me = lax.axis_index("tm")
    slots = REACH + 1
    has_next = r + 1 < groups
    has_prev = r > 0
    nxt = jnp.minimum(r + 1, groups - 1)
    prv = jnp.maximum(r - 1, 0)

    ch = w_mid_ref.shape[-1]
    k_all = 3 * ch
    for a in range(3):
        pltpu.make_async_copy(w_mid_ref.at[a], raw.at[a], raw_sem.at[a]).start()

    barrier = pltpu.get_barrier_semaphore()
    for t in range(members):

        @pl.when(me != t)
        def _():
            pl.semaphore_signal(barrier, inc=1, device_id=(r, jnp.int32(t)), device_id_type=MESH)

    @pl.when(has_prev & (me < REACH))
    def _():
        for t in range(members):
            pl.semaphore_signal(barrier, inc=1, device_id=(prv, jnp.int32(t)), device_id_type=MESH)

    mine = lat_ref[...].astype(F32)
    for u in range(lat_ref.shape[0]):
        stage[u] = mine[u : u + 1, :].astype(BF16)

    @pl.when(has_next)
    def _():
        pl.semaphore_wait(barrier, members - 1 + REACH)

    @pl.when(jnp.logical_not(has_next))
    def _():
        pl.semaphore_wait(barrier, members - 1)

    def within(t, sender):
        count = min(t, REACH) + 1
        return stage.at[pl.ds(t + 1 - count, count)], recv.at[sender, pl.ds(slots - count, count)]

    def across(t, sender):
        count = REACH - t
        return stage.at[pl.ds(members - count, count)], recv.at[sender, pl.ds(0, count)]

    def near_copy(t):
        src, dst = within(t, me)
        return pltpu.make_async_remote_copy(
            src_ref=src,
            dst_ref=dst,
            send_sem=send_sem.at[t],
            recv_sem=recv_sem.at[0, me],
            device_id=(r, jnp.int32(t)),
            device_id_type=MESH,
        )

    def far_copy(t):
        src, dst = across(t, me)
        return pltpu.make_async_remote_copy(
            src_ref=src,
            dst_ref=dst,
            send_sem=send_sem.at[members + t],
            recv_sem=recv_sem.at[1, me],
            device_id=(nxt, jnp.int32(t)),
            device_id_type=MESH,
        )

    @pl.when(has_next)
    def _():
        for t in range(REACH):
            far_copy(t).start()

    for t in range(members):

        @pl.when(me != t)
        def _():
            near_copy(t).start()

        @pl.when(me == t)
        def _():
            src, dst = within(t, t)
            own = pltpu.make_async_copy(src, dst, own_sem)
            own.start()

    chunk = 16
    for a in range(3):
        pltpu.make_async_copy(w_mid_ref.at[a], raw.at[a], raw_sem.at[a]).wait()

        def combine(n, carry):
            at = pl.multiple_of(n * chunk, chunk)
            for o in range(ch // 128):
                lane = pl.ds(o * 128, 128)
                w = [
                    [raw[a, p, q, pl.ds(at, chunk), lane].astype(F32) for q in range(3)]
                    for p in range(3)
                ]
                s = [w[0][q] + w[1][q] + w[2][q] for q in range(3)]

                def columns(t):
                    return ((t[0], t[1] + t[2]), (t[0] + t[1], t[2]))

                s_c, u_c, l_c = columns(s), columns(w[0]), columns(w[2])
                for b in range(2):
                    for v in range(2):
                        dst = pl.ds(pl.multiple_of(v * k_all + a * ch + at, chunk), chunk)
                        ws[b, dst, lane] = s_c[b][v].astype(BF16)
                        wd[b, dst, lane] = u_c[b][v].astype(BF16)
                        wd[b, dst, pl.ds(ch + o * 128, 128)] = l_c[b][v].astype(BF16)
            return carry

        lax.fori_loop(0, ch // chunk, combine, 0)

    for t in range(members):

        @pl.when(me == t)
        def _():
            for sender in range(members):
                src, dst = within(t, sender)
                sem = own_sem if sender == t else recv_sem.at[0, sender]
                pltpu.make_async_copy(src, dst, sem).wait()
            if t < REACH:

                @pl.when(has_prev)
                def _():
                    for sender in range(members):
                        src, dst = across(t, sender)
                        pltpu.make_async_copy(src, dst, recv_sem.at[1, sender]).wait()

                @pl.when(jnp.logical_not(has_prev))
                def _():
                    for sender in range(members):
                        recv[sender, 0 : REACH - t] = jnp.zeros(
                            (REACH - t,) + recv.shape[2:], recv.dtype
                        )

    rows = recv.shape[-1] // line
    for sender in range(members):
        for s in range(slots):
            piece = recv[sender, s].astype(F32)
            for n in range(rows):
                out_ref[s, pl.ds(sender * rows + n, 1), :] = piece[:, n * line : (n + 1) * line]

    for t in range(members):

        @pl.when(me != t)
        def _():
            near_copy(t).wait_send()

    @pl.when(has_next)
    def _():
        for t in range(REACH):
            far_copy(t).wait_send()


def exchange(latents, w_mid, groups, members, line):
    frames, feats = latents.shape
    rows = feats // line
    slots = REACH + 1
    ch = w_mid.shape[-1]
    vmem = pl.BlockSpec(memory_space=pltpu.VMEM)
    hbm = pl.BlockSpec(memory_space=pl.ANY)
    ws = (2, 6 * ch, ch)
    wd = (2, 6 * ch, 2 * ch)
    return pl.pallas_call(
        functools.partial(exchange_kernel, groups, members, line),
        out_shape=(
            jax.ShapeDtypeStruct((slots, rows * members, line), F32),
            jax.ShapeDtypeStruct(ws, BF16),
            jax.ShapeDtypeStruct(wd, BF16),
        ),
        in_specs=[vmem, hbm],
        out_specs=(vmem, vmem, vmem),
        scratch_shapes=[
            pltpu.VMEM((frames, 1, feats), BF16),
            pltpu.VMEM((members, slots, 1, feats), BF16),
            pltpu.VMEM(w_mid.shape, BF16),
            pltpu.SemaphoreType.DMA((members + REACH,)),
            pltpu.SemaphoreType.DMA((2, members)),
            pltpu.SemaphoreType.DMA,
            pltpu.SemaphoreType.DMA((3,)),
        ],
        compiler_params=pltpu.CompilerParams(
            collective_id=0, has_side_effects=True, vmem_limit_bytes=40 * 1024 * 1024
        ),
        name="exchange",
    )(latents, w_mid)


def decode_kernel(
    members, steps, ht, wt, c, ch,
    lengths_ref, x_ref, w_in_ref, b_in_ref, ws, wd, b_mid_ref, out_ref,
    lh, ld, hb, sl, wide,
):
    step = pl.program_id(0)
    pos = ht * wt
    k_all = 3 * ch
    per = 128 // ht
    frame = lax.axis_index("req") * members + lax.axis_index("tm")

    def request_of(f):
        end = jnp.int32(0)
        count = jnp.int32(0)
        for r in range(lengths_ref.shape[0]):
            end = end + lengths_ref[r]
            count = count + (f >= end).astype(jnp.int32)
        return count

    def linked(earlier, f):
        return ((earlier >= 0) & (request_of(earlier) == request_of(f))) | (earlier == f)

    @pl.when(step == 0)
    def _prologue():
        row_id = lax.broadcasted_iota(jnp.int32, (ht, wt * c), 0)
        quarter = lax.broadcasted_iota(jnp.int32, (c, 128), 1) // ht

        def spread(s, carry):
            x = jnp.where(frame - REACH + s >= 0, x_ref[s], 0.0)
            above = jnp.where(row_id == 0, 0.0, pltpu.roll(x, 1, 0))
            below = jnp.where(row_id == ht - 1, 0.0, pltpu.roll(x, ht - 1, 0))
            stacked = jnp.concatenate([above, x, below] + [jnp.zeros_like(x)] * (per - 3), axis=0)
            turned = stacked.T
            rolled = [turned] + [pltpu.roll(turned, ht * n, 1) for n in range(1, per)]
            zero = jnp.zeros((c, 128), F32)
            for di in range(3):
                for dj in range(3):
                    for jb in range(wt // per):
                        piece = zero
                        for jj in range(per):
                            j = jb * per + jj + dj - 1
                            if 0 <= j < wt:
                                part = rolled[(jj - di) % per][j * c : (j + 1) * c, :]
                                piece = jnp.where(quarter == jj, part, piece)
                        at = pl.multiple_of(s * 9 * c + (di * 3 + dj) * c, c)
                        sl[pl.ds(at, c), pl.ds(jb * 128, 128)] = piece.astype(BF16)
            return carry

        for s in range(REACH + 1):
            spread(s, 0)

        column = lax.broadcasted_iota(jnp.int32, (pos, 128), 0) % wt

        def first_layer(g, carry):
            f = frame - 2 + g
            taps = []
            for a in range(3):
                w = w_in_ref[a]
                taps.append(jnp.where(linked(f - 2 + a, f), w, jnp.zeros_like(w)))
            acc = lax.dot_general(
                sl[pl.ds(pl.multiple_of(g * 9 * c, c), 27 * c), :],
                jnp.concatenate(taps, 0),
                (((0,), (0,)), ((), ())),
                preferred_element_type=F32,
            )
            v = acc + b_in_ref[...][None, :]
            h = (v * (0.5 + 0.5 * jnp.tanh(0.5 * v))).astype(BF16).astype(F32)
            h = jnp.where(linked(f, frame), h, 0.0)
            for j in range(wt):
                for n in range(ch // 128):
                    part = h[j * ht : (j + 1) * ht, n * 128 : (n + 1) * 128]
                    hb[g, n, pl.ds(8 + j, ht, stride=wt), :] = part
            z = jnp.zeros((wt, 128), F32)
            rest = jnp.zeros((ld.shape[0] - pos - wt, 128), F32)
            for n in range(ch // 128):
                left = jnp.where(column == 0, 0.0, hb[g, n, pl.ds(7, pos), :])
                right = jnp.where(column == wt - 1, 0.0, hb[g, n, pl.ds(9, pos), :])
                for v_at, x in enumerate((left, hb[g, n, pl.ds(8, pos), :], right)):
                    lane = pl.ds(v_at * k_all + g * ch + n * 128, 128)
                    lh[:, lane] = x.astype(BF16)
                    d = jnp.concatenate([x, z, rest], 0) - jnp.concatenate([z, x, rest], 0)
                    ld[:, lane] = d.astype(BF16)
            return carry

        for g in range(3):
            first_layer(g, 0)


    lines = ht // steps
    m = lines * wt
    m_ext = m + 2 * 16
    row0 = pl.multiple_of(step * m, 16)
    for b in range(2):
        lane = pl.ds(b * k_all, 2 * k_all)
        ys = jnp.dot(lh[pl.ds(row0, m), lane], ws[b], preferred_element_type=F32) + b_mid_ref[...][None, :]
        yd = jnp.dot(ld[pl.ds(row0, m_ext), lane], wd[b], preferred_element_type=F32)
        y = (ys - yd[0:m, 0:ch], ys + yd[wt : wt + m, ch : 2 * ch])
        for i in range(lines):
            for a in range(2):
                for n in range(ch // 128):
                    wide[n, pl.ds((2 * i + a) * 2 * wt + b, wt, stride=2), :] = y[a][
                        i * wt : (i + 1) * wt, n * 128 : (n + 1) * 128
                    ]
    for i in range(2 * lines):
        for n in range(ch // 128):
            out_ref[i, :, n * 128 : (n + 1) * 128] = wide[n, pl.ds(i * 2 * wt, 2 * wt), :].astype(BF16)


def decode(x, lengths, w_in, b_in, ws, wd, b_mid, members):
    slots, ht, line = x.shape
    c, ch = w_in.shape[-2:]
    wt = line // c
    pos = ht * wt
    steps = 2
    m = pos // steps
    vmem = pl.BlockSpec(memory_space=pltpu.VMEM)
    return pl.pallas_call(
        functools.partial(decode_kernel, members, steps, ht, wt, c, ch),
        grid=(steps,),
        out_shape=jax.ShapeDtypeStruct((2 * ht, 2 * wt, ch), BF16),
        in_specs=[
            pl.BlockSpec(memory_space=pltpu.SMEM),
            vmem, vmem, vmem, vmem, vmem, vmem,
        ],
        out_specs=pl.BlockSpec((2 * ht // steps, 2 * wt, ch), lambda i: (i, 0, 0)),
        scratch_shapes=[
            pltpu.VMEM((pos, 9 * ch), BF16),
            pltpu.VMEM((pos + 32, 9 * ch), BF16),
            pltpu.VMEM((3, ch // 128, pos + 16, 128), F32),
            pltpu.VMEM((slots * 9 * c, pos), BF16),
            pltpu.VMEM((ch // 128, 4 * m, 128), F32),
        ],
        compiler_params=pltpu.CompilerParams(vmem_limit_bytes=40 * 1024 * 1024),
        name="decode",
    )(lengths, x, w_in.reshape(3, 9 * c, ch), b_in, ws, wd, b_mid)


def solution(mesh):
    groups, members = mesh.shape["req"], mesh.shape["tm"]

    def on_device(latents, lengths, w_in, b_in, w_mid, b_mid):
        c = w_in.shape[-2]
        line = 24 * c
        x, ws, wd = exchange(latents, w_mid, groups, members, line)
        return decode(x, lengths, w_in, b_in, ws, wd, b_mid, members)[None]

    in_specs = (P("req", "tm"), P(), P(), P(), P(), P())
    out_specs = P(("req", "tm"), None, None, None)
    return jax.shard_map(
        on_device, mesh=mesh, in_specs=in_specs, out_specs=out_specs, check_vma=False
    )
```

```python
import functools

import jax
import jax.numpy as jnp
from jax import lax
from jax.experimental import pallas as pl
from jax.experimental.pallas import tpu as pltpu
from jax.sharding import PartitionSpec as P

F32 = jnp.float32
BF16 = jnp.bfloat16
MESH = pl.DeviceIdType.MESH
REACH = 4


def exchange_kernel(
    groups, members, line,
    lat_ref, w_mid_ref, out_ref, ws, wd,
    stage, recv, raw, send_sem, recv_sem, own_sem, raw_sem,
):
    r = lax.axis_index("req")
    me = lax.axis_index("tm")
    slots = REACH + 1
    has_next = r + 1 < groups
    has_prev = r > 0
    nxt = jnp.minimum(r + 1, groups - 1)
    prv = jnp.maximum(r - 1, 0)

    ch = w_mid_ref.shape[-1]
    for a in range(3):
        pltpu.make_async_copy(w_mid_ref.at[a], raw.at[a], raw_sem.at[a]).start()

    barrier = pltpu.get_barrier_semaphore()
    for t in range(members):

        @pl.when(me != t)
        def _():
            pl.semaphore_signal(barrier, inc=1, device_id=(r, jnp.int32(t)), device_id_type=MESH)

    @pl.when(has_prev & (me < REACH))
    def _():
        for t in range(members):
            pl.semaphore_signal(barrier, inc=1, device_id=(prv, jnp.int32(t)), device_id_type=MESH)

    chunk = 16

    def combine_tap(a):
        pltpu.make_async_copy(w_mid_ref.at[a], raw.at[a], raw_sem.at[a]).wait()

        def combine(n, carry):
            at = pl.multiple_of(n * chunk, chunk)
            for o in range(ch // 128):
                lane = pl.ds(o * 128, 128)
                w = [
                    [raw[a, p, q, pl.ds(at, chunk), lane].astype(F32) for q in range(3)]
                    for p in range(3)
                ]
                s = [w[0][q] + w[1][q] + w[2][q] for q in range(3)]

                def columns(t):
                    return ((t[0], t[1] + t[2]), (t[0] + t[1], t[2]))

                s_c, u_c, l_c = columns(s), columns(w[0]), columns(w[2])
                for b in range(2):
                    for v in range(2):
                        dst = pl.ds(pl.multiple_of((2 * a + v) * ch + at, chunk), chunk)
                        ws[b, dst, lane] = s_c[b][v].astype(BF16)
                        wd[b, dst, lane] = u_c[b][v].astype(BF16)
                        wd[b, dst, pl.ds(ch + o * 128, 128)] = l_c[b][v].astype(BF16)
            return carry

        lax.fori_loop(0, ch // chunk, combine, 0)

    mine = lat_ref[...].astype(F32)
    for u in range(lat_ref.shape[0]):
        stage[u] = mine[u : u + 1, :].astype(BF16)
    combine_tap(0)

    @pl.when(has_next)
    def _():
        pl.semaphore_wait(barrier, members - 1 + REACH)

    @pl.when(jnp.logical_not(has_next))
    def _():
        pl.semaphore_wait(barrier, members - 1)

    def within(t, sender):
        count = min(t, REACH) + 1
        return stage.at[pl.ds(t + 1 - count, count)], recv.at[sender, pl.ds(slots - count, count)]

    def across(t, sender):
        count = REACH - t
        return stage.at[pl.ds(members - count, count)], recv.at[sender, pl.ds(0, count)]

    def near_copy(t):
        src, dst = within(t, me)
        return pltpu.make_async_remote_copy(
            src_ref=src,
            dst_ref=dst,
            send_sem=send_sem.at[t],
            recv_sem=recv_sem.at[0, me],
            device_id=(r, jnp.int32(t)),
            device_id_type=MESH,
        )

    def far_copy(t):
        src, dst = across(t, me)
        return pltpu.make_async_remote_copy(
            src_ref=src,
            dst_ref=dst,
            send_sem=send_sem.at[members + t],
            recv_sem=recv_sem.at[1, me],
            device_id=(nxt, jnp.int32(t)),
            device_id_type=MESH,
        )

    @pl.when(has_next)
    def _():
        for t in range(REACH):
            far_copy(t).start()

    for t in range(members):

        @pl.when(me != t)
        def _():
            near_copy(t).start()

        @pl.when(me == t)
        def _():
            src, dst = within(t, t)
            own = pltpu.make_async_copy(src, dst, own_sem)
            own.start()

    combine_tap(1)
    combine_tap(2)

    for t in range(members):

        @pl.when(me == t)
        def _():
            for sender in range(members):
                src, dst = within(t, sender)
                sem = own_sem if sender == t else recv_sem.at[0, sender]
                pltpu.make_async_copy(src, dst, sem).wait()
            if t < REACH:

                @pl.when(has_prev)
                def _():
                    for sender in range(members):
                        src, dst = across(t, sender)
                        pltpu.make_async_copy(src, dst, recv_sem.at[1, sender]).wait()

                @pl.when(jnp.logical_not(has_prev))
                def _():
                    for sender in range(members):
                        recv[sender, 0 : REACH - t] = jnp.zeros(
                            (REACH - t,) + recv.shape[2:], recv.dtype
                        )

    rows = recv.shape[-1] // line
    for sender in range(members):
        for s in range(slots):
            piece = recv[sender, s].astype(F32)
            for n in range(rows):
                out_ref[s, pl.ds(sender * rows + n, 1), :] = piece[:, n * line : (n + 1) * line]

    for t in range(members):

        @pl.when(me != t)
        def _():
            near_copy(t).wait_send()

    @pl.when(has_next)
    def _():
        for t in range(REACH):
            far_copy(t).wait_send()


def exchange(latents, w_mid, groups, members, line):
    frames, feats = latents.shape
    rows = feats // line
    slots = REACH + 1
    ch = w_mid.shape[-1]
    vmem = pl.BlockSpec(memory_space=pltpu.VMEM)
    hbm = pl.BlockSpec(memory_space=pl.ANY)
    ws = (2, 6 * ch, ch)
    wd = (2, 6 * ch, 2 * ch)
    return pl.pallas_call(
        functools.partial(exchange_kernel, groups, members, line),
        out_shape=(
            jax.ShapeDtypeStruct((slots, rows * members, line), F32),
            jax.ShapeDtypeStruct(ws, BF16),
            jax.ShapeDtypeStruct(wd, BF16),
        ),
        in_specs=[vmem, hbm],
        out_specs=(vmem, vmem, vmem),
        scratch_shapes=[
            pltpu.VMEM((frames, 1, feats), BF16),
            pltpu.VMEM((members, slots, 1, feats), BF16),
            pltpu.VMEM(w_mid.shape, BF16),
            pltpu.SemaphoreType.DMA((members + REACH,)),
            pltpu.SemaphoreType.DMA((2, members)),
            pltpu.SemaphoreType.DMA,
            pltpu.SemaphoreType.DMA((3,)),
        ],
        compiler_params=pltpu.CompilerParams(
            collective_id=0, has_side_effects=True, vmem_limit_bytes=40 * 1024 * 1024
        ),
        name="exchange",
    )(latents, w_mid)


def decode_kernel(
    members, ht, wt, c, ch,
    lengths_ref, x_ref, w_in_ref, b_in_ref, ws, wd, b_mid_ref, out_ref,
    lh, ld, hb, sl, acc_s, acc_d, wide, done, out_sem,
):
    pos = ht * wt
    per = 128 // ht
    frame = lax.axis_index("req") * members + lax.axis_index("tm")

    def request_of(f):
        end = jnp.int32(0)
        count = jnp.int32(0)
        for r in range(lengths_ref.shape[0]):
            end = end + lengths_ref[r]
            count = count + (f >= end).astype(jnp.int32)
        return count

    def linked(earlier, f):
        return ((earlier >= 0) & (request_of(earlier) == request_of(f))) | (earlier == f)

    row_id = lax.broadcasted_iota(jnp.int32, (ht, wt * c), 0)
    quarter = lax.broadcasted_iota(jnp.int32, (c, 128), 1) // ht
    column = lax.broadcasted_iota(jnp.int32, (pos, 128), 0) % wt

    def spread(s):
        x = jnp.where(frame - REACH + s >= 0, x_ref[s], 0.0)
        above = jnp.where(row_id == 0, 0.0, pltpu.roll(x, 1, 0))
        below = jnp.where(row_id == ht - 1, 0.0, pltpu.roll(x, ht - 1, 0))
        stacked = jnp.concatenate([above, x, below] + [jnp.zeros_like(x)] * (per - 3), axis=0)
        turned = stacked.T
        rolled = [turned] + [pltpu.roll(turned, ht * n, 1) for n in range(1, per)]
        zero = jnp.zeros((c, 128), F32)
        for di in range(3):
            for dj in range(3):
                for jb in range(wt // per):
                    piece = zero
                    for jj in range(per):
                        j = jb * per + jj + dj - 1
                        if 0 <= j < wt:
                            part = rolled[(jj - di) % per][j * c : (j + 1) * c, :]
                            piece = jnp.where(quarter == jj, part, piece)
                    at = s * 9 * c + (di * 3 + dj) * c
                    sl[pl.ds(at, c), pl.ds(jb * 128, 128)] = piece.astype(BF16)

    parts = 2
    cols = wt // parts

    def first_layer(g, part):
        f = frame - 2 + g
        taps = []
        for a in range(3):
            w = w_in_ref[a]
            taps.append(jnp.where(linked(f - 2 + a, f), w, jnp.zeros_like(w)))
        acc = lax.dot_general(
            sl[pl.ds(g * 9 * c, 27 * c), pl.ds(part * cols * ht, cols * ht)],
            jnp.concatenate(taps, 0),
            (((0,), (0,)), ((), ())),
            preferred_element_type=F32,
        )
        v = acc + b_in_ref[...][None, :]
        h = (v * (0.5 + 0.5 * jnp.tanh(0.5 * v))).astype(BF16).astype(F32)
        h = jnp.where(linked(f, frame), h, 0.0)
        for j in range(cols):
            for n in range(ch // 128):
                hb[g, n, pl.ds(8 + part * cols + j, ht, stride=wt), :] = h[
                    j * ht : (j + 1) * ht, n * 128 : (n + 1) * 128
                ]

    def operands(g, n):
        z = jnp.zeros((wt, 128), F32)
        rest = jnp.zeros((ld.shape[1] - pos - wt, 128), F32)
        left = jnp.where(column == 0, 0.0, hb[g, n, pl.ds(7, pos), :])
        right = jnp.where(column == wt - 1, 0.0, hb[g, n, pl.ds(9, pos), :])
        for v_at, x in enumerate((left, hb[g, n, pl.ds(8, pos), :], right)):
            lane = pl.ds(v_at * ch + n * 128, 128)
            lh[g, :, lane] = x.astype(BF16)
            d = jnp.concatenate([x, z, rest], 0) - jnp.concatenate([z, x, rest], 0)
            ld[g, :, lane] = d.astype(BF16)

    def multiply(g, b, lhs, rhs, acc, at, width):
        depth = pl.ds(b * ch, 2 * ch)
        out = pl.ds(at, width)
        got = jnp.dot(
            lhs[g, :, depth], rhs[b, pl.ds(g * 2 * ch, 2 * ch), out], preferred_element_type=F32
        )
        if g == 0:
            acc[b, :, out] = got
        else:
            acc[b, :, out] += got

    def products(g, b):
        jobs = []
        for lhs, rhs, acc in ((lh, ws, acc_s), (ld, wd, acc_d)):
            for at in range(0, rhs.shape[-1], 256):
                width = min(256, rhs.shape[-1] - at)
                jobs.append(functools.partial(multiply, g, b, lhs, rhs, acc, at, width))
        return jobs

    def build(g):
        jobs = [functools.partial(first_layer, g, part) for part in range(parts)]
        return jobs + [functools.partial(operands, g, n) for n in range(ch // 128)]

    def place(b, n):
        lane = pl.ds(n * 128, 128)
        ys = acc_s[b, :, lane] + b_mid_ref[lane][None, :]
        y = (
            ys - acc_d[b, pl.ds(0, pos), lane],
            ys + acc_d[b, pl.ds(wt, pos), pl.ds(ch + n * 128, 128)],
        )
        for i in range(ht):
            for a in range(2):
                wide[n, pl.ds((2 * i + a) * 2 * wt + b, wt, stride=2), :] = y[a][
                    i * wt : (i + 1) * wt, :
                ]

    def mix(first, second):
        for k in range(max(len(first), len(second))):
            for jobs in (first, second):
                if k < len(jobs):
                    jobs[k]()

    for s in range(3):
        spread(s)
    for job in build(0):
        job()
    spread(3)
    mix(products(0, 0) + products(0, 1), build(1) + [functools.partial(spread, 4)])
    mix(products(1, 0) + products(1, 1), build(2))
    for job in products(2, 0):
        job()
    mix(products(2, 1), [functools.partial(place, 0, n) for n in range(ch // 128)])

    for n in range(ch // 128):
        place(1, n)
    cuts = 4
    rows = 2 * ht // cuts
    puts = []
    for cut in range(cuts):
        for i in range(cut * rows, (cut + 1) * rows):
            for n in range(ch // 128):
                done[i, :, n * 128 : (n + 1) * 128] = wide[n, pl.ds(i * 2 * wt, 2 * wt), :].astype(BF16)
        part = pl.ds(cut * rows, rows)
        puts.append(pltpu.make_async_copy(done.at[part], out_ref.at[part], out_sem.at[cut]))
        puts[-1].start()
    for put in puts:
        put.wait()


def decode(x, lengths, w_in, b_in, ws, wd, b_mid, members):
    slots, ht, line = x.shape
    c, ch = w_in.shape[-2:]
    wt = line // c
    pos = ht * wt
    vmem = pl.BlockSpec(memory_space=pltpu.VMEM)
    return pl.pallas_call(
        functools.partial(decode_kernel, members, ht, wt, c, ch),
        out_shape=jax.ShapeDtypeStruct((2 * ht, 2 * wt, ch), BF16),
        in_specs=[
            pl.BlockSpec(memory_space=pltpu.SMEM),
            vmem, vmem, vmem, vmem, vmem, vmem,
        ],
        out_specs=pl.BlockSpec(memory_space=pl.ANY),
        scratch_shapes=[
            pltpu.VMEM((3, pos, 3 * ch), BF16),
            pltpu.VMEM((3, pos + 32, 3 * ch), BF16),
            pltpu.VMEM((3, ch // 128, pos + 16, 128), F32),
            pltpu.VMEM((slots * 9 * c, pos), BF16),
            pltpu.VMEM((2, pos, ch), F32),
            pltpu.VMEM((2, pos + 32, 2 * ch), F32),
            pltpu.VMEM((ch // 128, 4 * pos, 128), F32),
            pltpu.VMEM((2 * ht, 2 * wt, ch), BF16),
            pltpu.SemaphoreType.DMA((4,)),
        ],
        compiler_params=pltpu.CompilerParams(vmem_limit_bytes=40 * 1024 * 1024),
        name="decode",
    )(lengths, x, w_in.reshape(3, 9 * c, ch), b_in, ws, wd, b_mid)


def solution(mesh):
    groups, members = mesh.shape["req"], mesh.shape["tm"]

    def on_device(latents, lengths, w_in, b_in, w_mid, b_mid):
        c = w_in.shape[-2]
        line = 24 * c
        x, ws, wd = exchange(latents, w_mid, groups, members, line)
        return decode(x, lengths, w_in, b_in, ws, wd, b_mid, members)[None]

    in_specs = (P("req", "tm"), P(), P(), P(), P(), P())
    out_specs = P(("req", "tm"), None, None, None)
    return jax.shard_map(
        on_device, mesh=mesh, in_specs=in_specs, out_specs=out_specs, check_vma=False
    )
```

```python
import functools

import jax
import jax.numpy as jnp
from jax import lax
from jax.experimental import pallas as pl
from jax.experimental.pallas import tpu as pltpu
from jax.sharding import PartitionSpec as P

F32 = jnp.float32
BF16 = jnp.bfloat16
MESH = pl.DeviceIdType.MESH
REACH = 4


def exchange_kernel(
    groups, members, line,
    lat_ref, w_mid_ref, out_ref, ws, wd,
    stage, recv, raw, send_sem, recv_sem, own_sem, raw_sem,
):
    r = lax.axis_index("req")
    me = lax.axis_index("tm")
    slots = REACH + 1
    has_next = r + 1 < groups
    has_prev = r > 0
    nxt = jnp.minimum(r + 1, groups - 1)
    prv = jnp.maximum(r - 1, 0)

    ch = w_mid_ref.shape[-1]
    for a in range(3):
        pltpu.make_async_copy(w_mid_ref.at[a], raw.at[a], raw_sem.at[a]).start()

    barrier = pltpu.get_barrier_semaphore()
    for t in range(members):

        @pl.when(me != t)
        def _():
            pl.semaphore_signal(barrier, inc=1, device_id=(r, jnp.int32(t)), device_id_type=MESH)

    @pl.when(has_prev & (me < REACH))
    def _():
        for t in range(members):
            pl.semaphore_signal(barrier, inc=1, device_id=(prv, jnp.int32(t)), device_id_type=MESH)

    chunk = 16

    def combine_tap(a):
        pltpu.make_async_copy(w_mid_ref.at[a], raw.at[a], raw_sem.at[a]).wait()

        def combine(n, carry):
            at = pl.multiple_of(n * chunk, chunk)
            for o in range(ch // 128):
                lane = pl.ds(o * 128, 128)
                w = [
                    [raw[a, p, q, pl.ds(at, chunk), lane].astype(F32) for q in range(3)]
                    for p in range(3)
                ]
                s = [w[0][q] + w[1][q] + w[2][q] for q in range(3)]

                def columns(t):
                    return ((t[0], t[1] + t[2]), (t[0] + t[1], t[2]))

                s_c, u_c, l_c = columns(s), columns(w[0]), columns(w[2])
                for b in range(2):
                    for v in range(2):
                        dst = pl.ds(pl.multiple_of((2 * a + v) * ch + at, chunk), chunk)
                        ws[b, dst, lane] = s_c[b][v].astype(BF16)
                        wd[b, dst, lane] = u_c[b][v].astype(BF16)
                        wd[b, dst, pl.ds(ch + o * 128, 128)] = l_c[b][v].astype(BF16)
            return carry

        lax.fori_loop(0, ch // chunk, combine, 0)

    mine = lat_ref[...].astype(F32)
    for u in range(lat_ref.shape[0]):
        stage[u] = mine[u : u + 1, :].astype(BF16)

    @pl.when(has_next)
    def _():
        pl.semaphore_wait(barrier, members - 1 + REACH)

    @pl.when(jnp.logical_not(has_next))
    def _():
        pl.semaphore_wait(barrier, members - 1)

    def within(t, sender):
        count = min(t, REACH) + 1
        return stage.at[pl.ds(t + 1 - count, count)], recv.at[sender, pl.ds(slots - count, count)]

    def across(t, sender):
        count = REACH - t
        return stage.at[pl.ds(members - count, count)], recv.at[sender, pl.ds(0, count)]

    def near_copy(t):
        src, dst = within(t, me)
        return pltpu.make_async_remote_copy(
            src_ref=src,
            dst_ref=dst,
            send_sem=send_sem.at[t],
            recv_sem=recv_sem.at[0, me],
            device_id=(r, jnp.int32(t)),
            device_id_type=MESH,
        )

    def far_copy(t):
        src, dst = across(t, me)
        return pltpu.make_async_remote_copy(
            src_ref=src,
            dst_ref=dst,
            send_sem=send_sem.at[members + t],
            recv_sem=recv_sem.at[1, me],
            device_id=(nxt, jnp.int32(t)),
            device_id_type=MESH,
        )

    @pl.when(has_next)
    def _():
        for t in range(REACH):
            far_copy(t).start()

    for t in range(members):

        @pl.when(me != t)
        def _():
            near_copy(t).start()

        @pl.when(me == t)
        def _():
            src, dst = within(t, t)
            own = pltpu.make_async_copy(src, dst, own_sem)
            own.start()

    for a in range(3):
        combine_tap(a)

    for t in range(members):

        @pl.when(me == t)
        def _():
            for sender in range(members):
                src, dst = within(t, sender)
                sem = own_sem if sender == t else recv_sem.at[0, sender]
                pltpu.make_async_copy(src, dst, sem).wait()
            if t < REACH:

                @pl.when(has_prev)
                def _():
                    for sender in range(members):
                        src, dst = across(t, sender)
                        pltpu.make_async_copy(src, dst, recv_sem.at[1, sender]).wait()

                @pl.when(jnp.logical_not(has_prev))
                def _():
                    for sender in range(members):
                        recv[sender, 0 : REACH - t] = jnp.zeros(
                            (REACH - t,) + recv.shape[2:], recv.dtype
                        )

    rows = recv.shape[-1] // line
    for sender in range(members):
        for s in range(slots):
            piece = recv[sender, s].astype(F32)
            for n in range(rows):
                out_ref[s, pl.ds(sender * rows + n, 1), :] = piece[:, n * line : (n + 1) * line]

    for t in range(members):

        @pl.when(me != t)
        def _():
            near_copy(t).wait_send()

    @pl.when(has_next)
    def _():
        for t in range(REACH):
            far_copy(t).wait_send()


def exchange(latents, w_mid, groups, members, line):
    frames, feats = latents.shape
    rows = feats // line
    slots = REACH + 1
    ch = w_mid.shape[-1]
    vmem = pl.BlockSpec(memory_space=pltpu.VMEM)
    hbm = pl.BlockSpec(memory_space=pl.ANY)
    ws = (2, 6 * ch, ch)
    wd = (2, 6 * ch, 2 * ch)
    return pl.pallas_call(
        functools.partial(exchange_kernel, groups, members, line),
        out_shape=(
            jax.ShapeDtypeStruct((slots, rows * members, line), F32),
            jax.ShapeDtypeStruct(ws, BF16),
            jax.ShapeDtypeStruct(wd, BF16),
        ),
        in_specs=[vmem, hbm],
        out_specs=(vmem, vmem, vmem),
        scratch_shapes=[
            pltpu.VMEM((frames, 1, feats), BF16),
            pltpu.VMEM((members, slots, 1, feats), BF16),
            pltpu.VMEM(w_mid.shape, BF16),
            pltpu.SemaphoreType.DMA((members + REACH,)),
            pltpu.SemaphoreType.DMA((2, members)),
            pltpu.SemaphoreType.DMA,
            pltpu.SemaphoreType.DMA((3,)),
        ],
        compiler_params=pltpu.CompilerParams(
            collective_id=0, has_side_effects=True, vmem_limit_bytes=40 * 1024 * 1024
        ),
        name="exchange",
    )(latents, w_mid)


def decode_kernel(
    members, ht, wt, c, ch,
    lengths_ref, x_ref, w_in_ref, b_in_ref, ws, wd, b_mid_ref, out_ref,
    lh, ld, hb, sl, acc_s, acc_d, wide, done, out_sem,
):
    pos = ht * wt
    per = 128 // ht
    frame = lax.axis_index("req") * members + lax.axis_index("tm")

    def request_of(f):
        end = jnp.int32(0)
        count = jnp.int32(0)
        for r in range(lengths_ref.shape[0]):
            end = end + lengths_ref[r]
            count = count + (f >= end).astype(jnp.int32)
        return count

    def linked(earlier, f):
        return ((earlier >= 0) & (request_of(earlier) == request_of(f))) | (earlier == f)

    row_id = lax.broadcasted_iota(jnp.int32, (ht, wt * c), 0)
    quarter = lax.broadcasted_iota(jnp.int32, (c, 128), 1) // ht
    column = lax.broadcasted_iota(jnp.int32, (pos, 128), 0) % wt

    def spread(s):
        x = jnp.where(frame - REACH + s >= 0, x_ref[s], 0.0)
        above = jnp.where(row_id == 0, 0.0, pltpu.roll(x, 1, 0))
        below = jnp.where(row_id == ht - 1, 0.0, pltpu.roll(x, ht - 1, 0))
        stacked = jnp.concatenate([above, x, below] + [jnp.zeros_like(x)] * (per - 3), axis=0)
        turned = stacked.T
        rolled = [turned] + [pltpu.roll(turned, ht * n, 1) for n in range(1, per)]
        zero = jnp.zeros((c, 128), F32)
        for di in range(3):
            for dj in range(3):
                for jb in range(wt // per):
                    piece = zero
                    for jj in range(per):
                        j = jb * per + jj + dj - 1
                        if 0 <= j < wt:
                            part = rolled[(jj - di) % per][j * c : (j + 1) * c, :]
                            piece = jnp.where(quarter == jj, part, piece)
                    at = s * 9 * c + (di * 3 + dj) * c
                    sl[pl.ds(at, c), pl.ds(jb * 128, 128)] = piece.astype(BF16)

    parts = 2
    cols = wt // parts

    def first_layer(g, part):
        f = frame - 2 + g
        taps = []
        for a in range(3):
            w = w_in_ref[a]
            taps.append(jnp.where(linked(f - 2 + a, f), w, jnp.zeros_like(w)))
        acc = lax.dot_general(
            sl[pl.ds(g * 9 * c, 27 * c), pl.ds(part * cols * ht, cols * ht)],
            jnp.concatenate(taps, 0),
            (((0,), (0,)), ((), ())),
            preferred_element_type=F32,
        )
        v = acc + b_in_ref[...][None, :]
        h = (v * (0.5 + 0.5 * jnp.tanh(0.5 * v))).astype(BF16).astype(F32)
        h = jnp.where(linked(f, frame), h, 0.0)
        for j in range(cols):
            for n in range(ch // 128):
                hb[g, n, pl.ds(8 + part * cols + j, ht, stride=wt), :] = h[
                    j * ht : (j + 1) * ht, n * 128 : (n + 1) * 128
                ]

    def operands(g, n):
        z = jnp.zeros((wt, 128), F32)
        rest = jnp.zeros((ld.shape[1] - pos - wt, 128), F32)
        left = jnp.where(column == 0, 0.0, hb[g, n, pl.ds(7, pos), :])
        right = jnp.where(column == wt - 1, 0.0, hb[g, n, pl.ds(9, pos), :])
        for v_at, x in enumerate((left, hb[g, n, pl.ds(8, pos), :], right)):
            lane = pl.ds(v_at * ch + n * 128, 128)
            lh[g, :, lane] = x.astype(BF16)
            d = jnp.concatenate([x, z, rest], 0) - jnp.concatenate([z, x, rest], 0)
            ld[g, :, lane] = d.astype(BF16)

    def multiply(g, b, lhs, rhs, acc, at, width, rows):
        depth = pl.ds(b * ch, 2 * ch)
        out = pl.ds(at, width)
        got = jnp.dot(
            lhs[g, rows, depth], rhs[b, pl.ds(g * 2 * ch, 2 * ch), out], preferred_element_type=F32
        )
        if g == 0:
            acc[b, rows, out] = got
        else:
            acc[b, rows, out] += got

    half = pos // 2
    every = (pl.ds(0, pos), pl.ds(0, pos + 32))
    halves = (
        (pl.ds(0, half), pl.ds(0, half + 32)),
        (pl.ds(half, half), pl.ds(half + 32, half)),
    )

    def products(g, b, rows=every):
        jobs = []
        for lhs, rhs, acc, own in ((lh, ws, acc_s, rows[0]), (ld, wd, acc_d, rows[1])):
            for at in range(0, rhs.shape[-1], 256):
                width = min(256, rhs.shape[-1] - at)
                jobs.append(functools.partial(multiply, g, b, lhs, rhs, acc, at, width, own))
        return jobs

    def build(g):
        jobs = [functools.partial(first_layer, g, part) for part in range(parts)]
        return jobs + [functools.partial(operands, g, n) for n in range(ch // 128)]

    def place(b, n, at):
        lane = pl.ds(n * 128, 128)
        top = at * half
        ys = acc_s[b, pl.ds(top, half), lane] + b_mid_ref[lane][None, :]
        y = (
            ys - acc_d[b, pl.ds(top, half), lane],
            ys + acc_d[b, pl.ds(top + wt, half), pl.ds(ch + n * 128, 128)],
        )
        for i in range(ht // 2):
            for a in range(2):
                row = at * ht + 2 * i + a
                wide[n, pl.ds(row * 2 * wt + b, wt, stride=2), :] = y[a][i * wt : (i + 1) * wt, :]

    puts = []

    def finish(cut):
        rows = 2 * ht // 4
        for i in range(cut * rows, (cut + 1) * rows):
            for n in range(ch // 128):
                done[i, :, n * 128 : (n + 1) * 128] = wide[n, pl.ds(i * 2 * wt, 2 * wt), :].astype(BF16)
        part = pl.ds(cut * rows, rows)
        puts.append(pltpu.make_async_copy(done.at[part], out_ref.at[part], out_sem.at[cut]))
        puts[-1].start()

    def placing(at):
        return [functools.partial(place, b, n, at) for b in range(2) for n in range(ch // 128)]

    def mix(first, second):
        for k in range(max(len(first), len(second))):
            for jobs in (first, second):
                if k < len(jobs):
                    jobs[k]()

    for s in range(3):
        spread(s)
    for job in build(0):
        job()
    mix(
        products(0, 0) + products(0, 1),
        [functools.partial(spread, 3)] + build(1) + [functools.partial(spread, 4)],
    )
    mix(products(1, 0) + products(1, 1), build(2))
    for job in products(2, 0, halves[0]) + products(2, 1, halves[0]):
        job()
    mix(
        products(2, 0, halves[1]) + products(2, 1, halves[1]),
        placing(0) + [functools.partial(finish, cut) for cut in range(2)],
    )
    for job in placing(1):
        job()
    for cut in range(2, 4):
        finish(cut)
    for put in puts:
        put.wait()


def decode(x, lengths, w_in, b_in, ws, wd, b_mid, members):
    slots, ht, line = x.shape
    c, ch = w_in.shape[-2:]
    wt = line // c
    pos = ht * wt
    vmem = pl.BlockSpec(memory_space=pltpu.VMEM)
    return pl.pallas_call(
        functools.partial(decode_kernel, members, ht, wt, c, ch),
        out_shape=jax.ShapeDtypeStruct((2 * ht, 2 * wt, ch), BF16),
        in_specs=[
            pl.BlockSpec(memory_space=pltpu.SMEM),
            vmem, vmem, vmem, vmem, vmem, vmem,
        ],
        out_specs=pl.BlockSpec(memory_space=pl.ANY),
        scratch_shapes=[
            pltpu.VMEM((3, pos, 3 * ch), BF16),
            pltpu.VMEM((3, pos + 32, 3 * ch), BF16),
            pltpu.VMEM((3, ch // 128, pos + 16, 128), F32),
            pltpu.VMEM((slots * 9 * c, pos), BF16),
            pltpu.VMEM((2, pos, ch), F32),
            pltpu.VMEM((2, pos + 32, 2 * ch), F32),
            pltpu.VMEM((ch // 128, 4 * pos, 128), F32),
            pltpu.VMEM((2 * ht, 2 * wt, ch), BF16),
            pltpu.SemaphoreType.DMA((4,)),
        ],
        compiler_params=pltpu.CompilerParams(vmem_limit_bytes=40 * 1024 * 1024),
        name="decode",
    )(lengths, x, w_in.reshape(3, 9 * c, ch), b_in, ws, wd, b_mid)


def solution(mesh):
    groups, members = mesh.shape["req"], mesh.shape["tm"]

    def on_device(latents, lengths, w_in, b_in, w_mid, b_mid):
        c = w_in.shape[-2]
        line = 24 * c
        x, ws, wd = exchange(latents, w_mid, groups, members, line)
        return decode(x, lengths, w_in, b_in, ws, wd, b_mid, members)[None]

    in_specs = (P("req", "tm"), P(), P(), P(), P(), P())
    out_specs = P(("req", "tm"), None, None, None)
    return jax.shard_map(
        on_device, mesh=mesh, in_specs=in_specs, out_specs=out_specs, check_vma=False
    )
```

```python
import functools

import jax
import jax.numpy as jnp
from jax import lax
from jax.experimental import pallas as pl
from jax.experimental.pallas import tpu as pltpu
from jax.sharding import PartitionSpec as P

F32 = jnp.float32
BF16 = jnp.bfloat16
MESH = pl.DeviceIdType.MESH
REACH = 4


def exchange_kernel(
    groups, members, line,
    lat_ref, w_mid_ref, out_ref, ws, wd,
    stage, recv, raw, send_sem, recv_sem, own_sem, raw_sem,
):
    r = lax.axis_index("req")
    me = lax.axis_index("tm")
    slots = REACH + 1
    has_next = r + 1 < groups
    has_prev = r > 0
    nxt = jnp.minimum(r + 1, groups - 1)
    prv = jnp.maximum(r - 1, 0)

    ch = w_mid_ref.shape[-1]
    for a in range(3):
        pltpu.make_async_copy(w_mid_ref.at[a], raw.at[a], raw_sem.at[a]).start()

    barrier = pltpu.get_barrier_semaphore()
    for t in range(members):

        @pl.when(me != t)
        def _():
            pl.semaphore_signal(barrier, inc=1, device_id=(r, jnp.int32(t)), device_id_type=MESH)

    @pl.when(has_prev & (me < REACH))
    def _():
        for t in range(members):
            pl.semaphore_signal(barrier, inc=1, device_id=(prv, jnp.int32(t)), device_id_type=MESH)

    chunk = 16

    def combine_tap(a):
        pltpu.make_async_copy(w_mid_ref.at[a], raw.at[a], raw_sem.at[a]).wait()

        def combine(n, carry):
            at = pl.multiple_of(n * chunk, chunk)
            for o in range(ch // 128):
                lane = pl.ds(o * 128, 128)
                w = [
                    [raw[a, p, q, pl.ds(at, chunk), lane].astype(F32) for q in range(3)]
                    for p in range(3)
                ]
                s = [w[0][q] + w[1][q] + w[2][q] for q in range(3)]

                def columns(t):
                    return ((t[0], t[1] + t[2]), (t[0] + t[1], t[2]))

                s_c, u_c, l_c = columns(s), columns(w[0]), columns(w[2])
                for b in range(2):
                    for v in range(2):
                        dst = pl.ds(pl.multiple_of((2 * a + v) * ch + at, chunk), chunk)
                        ws[b, dst, lane] = s_c[b][v].astype(BF16)
                        wd[b, dst, lane] = u_c[b][v].astype(BF16)
                        wd[b, dst, pl.ds(ch + o * 128, 128)] = l_c[b][v].astype(BF16)
            return carry

        lax.fori_loop(0, ch // chunk, combine, 0)

    mine = lat_ref[...].astype(F32)
    for u in range(lat_ref.shape[0]):
        stage[u] = mine[u : u + 1, :].astype(BF16)

    @pl.when(has_next)
    def _():
        pl.semaphore_wait(barrier, members - 1 + REACH)

    @pl.when(jnp.logical_not(has_next))
    def _():
        pl.semaphore_wait(barrier, members - 1)

    def within(t, sender):
        count = min(t, REACH) + 1
        return stage.at[pl.ds(t + 1 - count, count)], recv.at[sender, pl.ds(slots - count, count)]

    def across(t, sender):
        count = REACH - t
        return stage.at[pl.ds(members - count, count)], recv.at[sender, pl.ds(0, count)]

    def near_copy(t):
        src, dst = within(t, me)
        return pltpu.make_async_remote_copy(
            src_ref=src,
            dst_ref=dst,
            send_sem=send_sem.at[t],
            recv_sem=recv_sem.at[0, me],
            device_id=(r, jnp.int32(t)),
            device_id_type=MESH,
        )

    def far_copy(t):
        src, dst = across(t, me)
        return pltpu.make_async_remote_copy(
            src_ref=src,
            dst_ref=dst,
            send_sem=send_sem.at[members + t],
            recv_sem=recv_sem.at[1, me],
            device_id=(nxt, jnp.int32(t)),
            device_id_type=MESH,
        )

    @pl.when(has_next)
    def _():
        for t in range(REACH):
            far_copy(t).start()

    for t in range(members):

        @pl.when(me != t)
        def _():
            near_copy(t).start()

        @pl.when(me == t)
        def _():
            src, dst = within(t, t)
            own = pltpu.make_async_copy(src, dst, own_sem)
            own.start()

    for a in range(3):
        combine_tap(a)

    for t in range(members):

        @pl.when(me == t)
        def _():
            for sender in range(members):
                src, dst = within(t, sender)
                sem = own_sem if sender == t else recv_sem.at[0, sender]
                pltpu.make_async_copy(src, dst, sem).wait()
            if t < REACH:

                @pl.when(has_prev)
                def _():
                    for sender in range(members):
                        src, dst = across(t, sender)
                        pltpu.make_async_copy(src, dst, recv_sem.at[1, sender]).wait()

                @pl.when(jnp.logical_not(has_prev))
                def _():
                    for sender in range(members):
                        recv[sender, 0 : REACH - t] = jnp.zeros(
                            (REACH - t,) + recv.shape[2:], recv.dtype
                        )

    rows = recv.shape[-1] // line
    for sender in range(members):
        for s in range(slots):
            piece = recv[sender, s].astype(F32)
            for n in range(rows):
                out_ref[s, pl.ds(sender * rows + n, 1), :] = piece[:, n * line : (n + 1) * line]

    for t in range(members):

        @pl.when(me != t)
        def _():
            near_copy(t).wait_send()

    @pl.when(has_next)
    def _():
        for t in range(REACH):
            far_copy(t).wait_send()


def exchange(latents, w_mid, groups, members, line):
    frames, feats = latents.shape
    rows = feats // line
    slots = REACH + 1
    ch = w_mid.shape[-1]
    vmem = pl.BlockSpec(memory_space=pltpu.VMEM)
    hbm = pl.BlockSpec(memory_space=pl.ANY)
    ws = (2, 6 * ch, ch)
    wd = (2, 6 * ch, 2 * ch)
    return pl.pallas_call(
        functools.partial(exchange_kernel, groups, members, line),
        out_shape=(
            jax.ShapeDtypeStruct((slots, rows * members, line), F32),
            jax.ShapeDtypeStruct(ws, BF16),
            jax.ShapeDtypeStruct(wd, BF16),
        ),
        in_specs=[vmem, hbm],
        out_specs=(vmem, vmem, vmem),
        scratch_shapes=[
            pltpu.VMEM((frames, 1, feats), BF16),
            pltpu.VMEM((members, slots, 1, feats), BF16),
            pltpu.VMEM(w_mid.shape, BF16),
            pltpu.SemaphoreType.DMA((members + REACH,)),
            pltpu.SemaphoreType.DMA((2, members)),
            pltpu.SemaphoreType.DMA,
            pltpu.SemaphoreType.DMA((3,)),
        ],
        compiler_params=pltpu.CompilerParams(
            collective_id=0, has_side_effects=True, vmem_limit_bytes=40 * 1024 * 1024
        ),
        name="exchange",
    )(latents, w_mid)


def decode_kernel(
    members, ht, wt, c, ch,
    lengths_ref, x_ref, w_in_ref, b_in_ref, ws, wd, b_mid_ref, out_ref,
    lh, ld, hb, sl, acc_s, acc_d, wide, done, out_sem,
):
    pos = ht * wt
    per = 128 // ht
    frame = lax.axis_index("req") * members + lax.axis_index("tm")

    def request_of(f):
        end = jnp.int32(0)
        count = jnp.int32(0)
        for r in range(lengths_ref.shape[0]):
            end = end + lengths_ref[r]
            count = count + (f >= end).astype(jnp.int32)
        return count

    def linked(earlier, f):
        return ((earlier >= 0) & (request_of(earlier) == request_of(f))) | (earlier == f)

    row_id = lax.broadcasted_iota(jnp.int32, (ht, wt * c), 0)
    quarter = lax.broadcasted_iota(jnp.int32, (c, 128), 1) // ht
    column = lax.broadcasted_iota(jnp.int32, (pos, 128), 0) % wt

    def spread(s):
        x = jnp.where(frame - REACH + s >= 0, x_ref[s], 0.0)
        above = jnp.where(row_id == 0, 0.0, pltpu.roll(x, 1, 0))
        below = jnp.where(row_id == ht - 1, 0.0, pltpu.roll(x, ht - 1, 0))
        stacked = jnp.concatenate([above, x, below] + [jnp.zeros_like(x)] * (per - 3), axis=0)
        turned = stacked.T
        rolled = [turned] + [pltpu.roll(turned, ht * n, 1) for n in range(1, per)]
        zero = jnp.zeros((c, 128), F32)
        for di in range(3):
            for dj in range(3):
                for jb in range(wt // per):
                    piece = zero
                    for jj in range(per):
                        j = jb * per + jj + dj - 1
                        if 0 <= j < wt:
                            part = rolled[(jj - di) % per][j * c : (j + 1) * c, :]
                            piece = jnp.where(quarter == jj, part, piece)
                    at = s * 9 * c + (di * 3 + dj) * c
                    sl[pl.ds(at, c), pl.ds(jb * 128, 128)] = piece.astype(BF16)

    parts = 2
    cols = wt // parts

    def first_layer(g, part):
        f = frame - 2 + g
        taps = []
        for a in range(3):
            w = w_in_ref[a]
            taps.append(jnp.where(linked(f - 2 + a, f), w, jnp.zeros_like(w)))
        acc = lax.dot_general(
            sl[pl.ds(g * 9 * c, 27 * c), pl.ds(part * cols * ht, cols * ht)],
            jnp.concatenate(taps, 0),
            (((0,), (0,)), ((), ())),
            preferred_element_type=F32,
        )
        v = acc + b_in_ref[...][None, :]
        h = (v * (0.5 + 0.5 * jnp.tanh(0.5 * v))).astype(BF16).astype(F32)
        h = jnp.where(linked(f, frame), h, 0.0)
        for j in range(cols):
            for n in range(ch // 128):
                hb[g, n, pl.ds(8 + part * cols + j, ht, stride=wt), :] = h[
                    j * ht : (j + 1) * ht, n * 128 : (n + 1) * 128
                ]

    def operands(g, n):
        z = jnp.zeros((wt, 128), F32)
        rest = jnp.zeros((ld.shape[1] - pos - wt, 128), F32)
        left = jnp.where(column == 0, 0.0, hb[g, n, pl.ds(7, pos), :])
        right = jnp.where(column == wt - 1, 0.0, hb[g, n, pl.ds(9, pos), :])
        for v_at, x in enumerate((left, hb[g, n, pl.ds(8, pos), :], right)):
            lane = pl.ds(v_at * ch + n * 128, 128)
            lh[g, :, lane] = x.astype(BF16)
            d = jnp.concatenate([x, z, rest], 0) - jnp.concatenate([z, x, rest], 0)
            ld[g, :, lane] = d.astype(BF16)

    def multiply(g, b, lhs, rhs, acc, at, width, rows):
        depth = pl.ds(b * ch, 2 * ch)
        out = pl.ds(at, width)
        got = jnp.dot(
            lhs[g, rows, depth], rhs[b, pl.ds(g * 2 * ch, 2 * ch), out], preferred_element_type=F32
        )
        if g == 0:
            acc[b, rows, out] = got
        else:
            acc[b, rows, out] += got

    half = pos // 2
    every = (pl.ds(0, pos), pl.ds(0, pos + 32))
    halves = (
        (pl.ds(0, half), pl.ds(0, half + 32)),
        (pl.ds(half, half), pl.ds(half + 32, half)),
    )

    def products(g, b, rows=every):
        jobs = []
        for lhs, rhs, acc, own in ((lh, ws, acc_s, rows[0]), (ld, wd, acc_d, rows[1])):
            jobs.append(functools.partial(multiply, g, b, lhs, rhs, acc, 0, rhs.shape[-1], own))
        return jobs

    def build(g):
        jobs = [functools.partial(first_layer, g, part) for part in range(parts)]
        return jobs + [functools.partial(operands, g, n) for n in range(ch // 128)]

    def place(b, n, at):
        lane = pl.ds(n * 128, 128)
        top = at * half
        ys = acc_s[b, pl.ds(top, half), lane] + b_mid_ref[lane][None, :]
        y = (
            ys - acc_d[b, pl.ds(top, half), lane],
            ys + acc_d[b, pl.ds(top + wt, half), pl.ds(ch + n * 128, 128)],
        )
        for i in range(ht // 2):
            for a in range(2):
                row = at * ht + 2 * i + a
                wide[n, pl.ds(row * 2 * wt + b, wt, stride=2), :] = y[a][i * wt : (i + 1) * wt, :]

    puts = []

    def finish(cut):
        rows = 2 * ht // 4
        for i in range(cut * rows, (cut + 1) * rows):
            for n in range(ch // 128):
                done[i, :, n * 128 : (n + 1) * 128] = wide[n, pl.ds(i * 2 * wt, 2 * wt), :].astype(BF16)
        part = pl.ds(cut * rows, rows)
        puts.append(pltpu.make_async_copy(done.at[part], out_ref.at[part], out_sem.at[cut]))
        puts[-1].start()

    def placing(at):
        return [functools.partial(place, b, n, at) for b in range(2) for n in range(ch // 128)]

    def mix(first, second):
        for k in range(max(len(first), len(second))):
            for jobs in (first, second):
                if k < len(jobs):
                    jobs[k]()

    for s in range(3):
        spread(s)
    for job in build(0):
        job()
    mix(
        products(0, 0) + products(0, 1),
        [functools.partial(spread, 3)] + build(1) + [functools.partial(spread, 4)],
    )
    mix(products(1, 0) + products(1, 1), build(2))
    for job in products(2, 0, halves[0]) + products(2, 1, halves[0]):
        job()
    mix(
        products(2, 0, halves[1]) + products(2, 1, halves[1]),
        placing(0) + [functools.partial(finish, cut) for cut in range(2)],
    )
    for job in placing(1):
        job()
    for cut in range(2, 4):
        finish(cut)
    for put in puts:
        put.wait()


def decode(x, lengths, w_in, b_in, ws, wd, b_mid, members):
    slots, ht, line = x.shape
    c, ch = w_in.shape[-2:]
    wt = line // c
    pos = ht * wt
    vmem = pl.BlockSpec(memory_space=pltpu.VMEM)
    return pl.pallas_call(
        functools.partial(decode_kernel, members, ht, wt, c, ch),
        out_shape=jax.ShapeDtypeStruct((2 * ht, 2 * wt, ch), BF16),
        in_specs=[
            pl.BlockSpec(memory_space=pltpu.SMEM),
            vmem, vmem, vmem, vmem, vmem, vmem,
        ],
        out_specs=pl.BlockSpec(memory_space=pl.ANY),
        scratch_shapes=[
            pltpu.VMEM((3, pos, 3 * ch), BF16),
            pltpu.VMEM((3, pos + 32, 3 * ch), BF16),
            pltpu.VMEM((3, ch // 128, pos + 16, 128), F32),
            pltpu.VMEM((slots * 9 * c, pos), BF16),
            pltpu.VMEM((2, pos, ch), F32),
            pltpu.VMEM((2, pos + 32, 2 * ch), F32),
            pltpu.VMEM((ch // 128, 4 * pos, 128), F32),
            pltpu.VMEM((2 * ht, 2 * wt, ch), BF16),
            pltpu.SemaphoreType.DMA((4,)),
        ],
        compiler_params=pltpu.CompilerParams(vmem_limit_bytes=40 * 1024 * 1024),
        name="decode",
    )(lengths, x, w_in.reshape(3, 9 * c, ch), b_in, ws, wd, b_mid)


def solution(mesh):
    groups, members = mesh.shape["req"], mesh.shape["tm"]

    def on_device(latents, lengths, w_in, b_in, w_mid, b_mid):
        c = w_in.shape[-2]
        line = 24 * c
        x, ws, wd = exchange(latents, w_mid, groups, members, line)
        return decode(x, lengths, w_in, b_in, ws, wd, b_mid, members)[None]

    in_specs = (P("req", "tm"), P(), P(), P(), P(), P())
    out_specs = P(("req", "tm"), None, None, None)
    return jax.shard_map(
        on_device, mesh=mesh, in_specs=in_specs, out_specs=out_specs, check_vma=False
    )
```
